512 devices in a mesh: row: 32 (over x, y), col: 16 (over z, core).
Axes of the slice: x: 4, y: 8, z: 8, core: 2. Of those that a mesh axis runs over, the one named last changes fastest.
Arguments:
- eigvecs: float32 [131072, 2048], P('row', 'col'), may hold values from -6 to 6
- householder: float32 [2, 131072, 256], P(None, 'row', 'col'), may hold values from -4 to 4, as said below
Outputs:
- backvecs: float32 [131072, 2048], P('row', 'col')
The draws below stay inside these ranges and needn't reach their ends.
Inputs may be any that keep to these rules, and one draw needn't show every extreme that they name: Every entry of householder has magnitude at least 0.5.
All inputs are finite; a program needn't handle non-finite values.
Results may differ from the reference program's by a relative error of at most 0.0001.
Values sent between devices are 32-bit elements; how exact they have to be, the bound alone decides.
No kernel may reach another device: no remote copies, remote signals or barrier semaphores. Data moves between devices by JAX's collectives and lax.ppermute only.
A program may use at most 64 MiB of HBM per device.

```python
import jax
import jax.numpy as jnp
from jax import lax

NB = 256
BLOCKS = 2
N = 131072
NE = 2048


def draw_householder(key, part):
    key = jax.random.fold_in(key, 7)
    sign_key, size_key = jax.random.split(key)
    shape = (BLOCKS, N, NB)
    signs = jnp.where(jax.random.bernoulli(sign_key, 0.5, shape), 1.0, -1.0)
    magnitude = jax.random.uniform(size_key, shape, jnp.float32, 0.5, 1.5)
    return (signs * magnitude).astype(jnp.float32)


def block_levels(rng, dims, shards, least, high):
    gain = 1.0
    for dim, shards_of in shards:
        heights = jax.random.uniform(jax.random.fold_in(jax.random.fold_in(rng, 6), dim), (shards_of,), jnp.float32, least / len(shards), high / len(shards))
        gain = gain * jnp.repeat(jnp.exp(heights), dims[dim] // shards_of).reshape((-1,) + (1,) * (len(dims) - 1 - dim))
    return gain


def centred(key, extent, scale, limit, pieces=(), kind=jnp.bfloat16):
    factor_of = block_levels(key, extent, pieces, -0.22, 0.18) if pieces else 1.0
    array = jax.random.normal(key, extent, jnp.float32) * scale * factor_of
    return jnp.minimum(jnp.maximum(array, -limit), limit).astype(kind)


def setup_inputs(seed: int = 0) -> dict:
    key_list = jax.random.split(jax.random.key(seed), 3)
    eigvecs = centred(key_list[0], (N, NE), 1.0, 6.0, ((0, 32), (1, 16)), jnp.float32)
    householder = draw_householder(jax.random.fold_in(key_list[2], 71), 0)
    return dict(eigvecs=eigvecs, householder=householder)


def reference(eigvecs, householder):
    current = eigvecs
    for block in range(BLOCKS - 1, -1, -1):
        panel = householder[block]
        gram = jnp.dot(panel.T.astype(jnp.float32), panel.astype(jnp.float32), precision=lax.Precision.HIGHEST, preferred_element_type=jnp.float32)
        inv_factor = jnp.triu(gram, 1) + jnp.diag(0.5 * jnp.diag(gram))
        project = jnp.dot(panel.T.astype(jnp.float32), current.astype(jnp.float32), precision=lax.Precision.HIGHEST, preferred_element_type=jnp.float32)
        coef = lax.linalg.triangular_solve(inv_factor, project, left_side=True, lower=False)
        current = current - jnp.dot(panel.astype(jnp.float32), coef.astype(jnp.float32), precision=lax.Precision.HIGHEST, preferred_element_type=jnp.float32)
    return current
```

```python
import jax
import jax.numpy as jnp
from jax import lax
from jax.experimental import pallas as pl
from jax.experimental.pallas import tpu as pltpu
from jax.sharding import PartitionSpec as P

F32 = jnp.float32
BF16 = jnp.bfloat16
CHIPS = 8
ROWS = 4096
COLS = 128
NV = 512
STEP = 512
VMEM = 56 * 1024 * 1024
ARRIVAL = (0, 1, -1, -2, 2, 3, -3, -4)
GRAM_BLOCKS = (
    ((0, 0), (0, 1), (0, 2), (0, 3), (1, 1)),
    ((1, 2), (1, 3), (2, 2), (2, 3), (3, 3)),
)


def split(value):
    high = value.astype(BF16)
    low = (value - high.astype(F32)).astype(BF16)
    return high, low


def nt(left, right):
    return lax.dot_general(left, right, (((1,), (1,)), ((), ())), preferred_element_type=F32)


def nn(left, right):
    return lax.dot_general(left, right, (((1,), (0,)), ((), ())), preferred_element_type=F32)


def hidot(left, right):
    return jnp.dot(left, right, precision=lax.Precision.HIGHEST, preferred_element_type=F32)


def products_kernel(place, *refs):
    pieces = refs[:8]
    c_ref, vhi, vlo, out, proj, gram = refs[8:]
    step = pl.program_id(0)

    @pl.when(step == 0)
    def _():
        proj[...] = jnp.zeros_like(proj)
        gram[...] = jnp.zeros_like(gram)

    for piece in range(8):
        for half in range(2):
            for block in range(2):
                first = half * 32 + block * 16
                high, low = split(pieces[piece][first : first + 16, :])
                at = pl.ds(pl.multiple_of(place[piece * 2 + half] + block * 256, 16), 16)
                vhi[at, :] = high
                vlo[at, :] = low
    chi, clo = split(c_ref[...])
    both = nn(vhi[...], jnp.concatenate([chi, clo], axis=1))
    proj[...] += both[:, :COLS] + both[:, COLS:] + nn(vlo[...], chi)
    for index in range(5):
        left = pl.ds(pl.multiple_of(place[16 + 2 * index], 128), 128)
        right = pl.ds(pl.multiple_of(place[17 + 2 * index], 128), 128)
        lhi, llo = vhi[left, :], vlo[left, :]
        rhi, rlo = vhi[right, :], vlo[right, :]
        gram[index * 128 : index * 128 + 128, :] += nt(lhi, rhi) + nt(lhi, rlo) + nt(llo, rhi)

    @pl.when(step == pl.num_programs(0) - 1)
    def _():
        out[:, :16, :] = proj[...].reshape(32, 16, COLS)
        out[:, 16:, :] = gram[...].reshape(32, 24, COLS)


def products(place, pieces, current):
    steps = ROWS // STEP
    return pl.pallas_call(
        products_kernel,
        grid=(steps,),
        in_specs=[pl.BlockSpec(memory_space=pltpu.SMEM)]
        + [pl.BlockSpec((64, STEP), lambda k: (0, k))] * 8
        + [pl.BlockSpec((STEP, COLS), lambda k: (k, 0))],
        out_specs=[
            pl.BlockSpec((NV, STEP), lambda k: (0, k)),
            pl.BlockSpec((NV, STEP), lambda k: (0, k)),
            pl.BlockSpec((32, 40, COLS), lambda k: (0, 0, 0)),
        ],
        out_shape=[
            jax.ShapeDtypeStruct((NV, ROWS), BF16),
            jax.ShapeDtypeStruct((NV, ROWS), BF16),
            jax.ShapeDtypeStruct((32, 40, COLS), F32),
        ],
        scratch_shapes=[pltpu.VMEM((NV, COLS), F32), pltpu.VMEM((768, 128), F32)],
        compiler_params=pltpu.CompilerParams(vmem_limit_bytes=VMEM),
        name="products",
    )(place, *pieces, current)


def invert_unit(nilpot):
    row = lax.broadcasted_iota(jnp.int32, (128, 128), 0)
    col = lax.broadcasted_iota(jnp.int32, (128, 128), 1)
    eye = (row == col).astype(F32)
    near = [jnp.where(row // 4 == col // 4, n, 0.0) for n in nilpot]
    square = [hidot(n, n) for n in near]
    inverse = [hidot(eye - n, eye + s) for n, s in zip(near, square)]
    size = 4
    while size < 128:
        pair = (row // (2 * size) == col // (2 * size)) & (row // size != col // size)
        right = [hidot(jnp.where(pair, n, 0.0), r) for n, r in zip(nilpot, inverse)]
        inverse = [r - hidot(r, t) for r, t in zip(inverse, right)]
        size *= 2
    return inverse


def solve_kernel(core, mine, other, xhi, xlo):
    zero = core[0] == 0
    gram = {}
    for which in range(2):
        flat = jnp.where(zero == (which == 0), mine[:, 16:, :], other[...]).reshape(768, 128)
        for index, at in enumerate(GRAM_BLOCKS[which]):
            gram[at] = flat[index * 128 : index * 128 + 128]
    project = mine[:, :16, :].reshape(NV, COLS)
    row = lax.broadcasted_iota(jnp.int32, (128, 128), 0)
    col = lax.broadcasted_iota(jnp.int32, (128, 128), 1)
    scale = [2.0 / jnp.sum(jnp.where(row == col, gram[i, i], 0.0), axis=1, keepdims=True) for i in range(4)]
    inverse = invert_unit([jnp.where(row < col, gram[i, i] * scale[i], 0.0) for i in range(4)])
    coef = [None] * 4
    for i in range(3, -1, -1):
        rhs = project[i * 128 : i * 128 + 128]
        if i < 3:
            panel = jnp.concatenate([gram[i, j] for j in range(i + 1, 4)], axis=1)
            rhs = rhs - hidot(panel, jnp.concatenate(coef[i + 1 :], axis=0))
        coef[i] = hidot(inverse[i], rhs * scale[i])
    high, low = split(jnp.concatenate(coef, axis=0).T)
    xhi[...] = high
    xlo[...] = low


def solve(core, mine, other):
    return pl.pallas_call(
        solve_kernel,
        in_specs=[pl.BlockSpec(memory_space=pltpu.SMEM)] + [pl.BlockSpec(memory_space=pltpu.VMEM)] * 2,
        out_specs=[pl.BlockSpec(memory_space=pltpu.VMEM)] * 2,
        out_shape=[jax.ShapeDtypeStruct((COLS, NV), BF16)] * 2,
        compiler_params=pltpu.CompilerParams(vmem_limit_bytes=VMEM),
        name="solve",
    )(core, mine, other)


def update_kernel(c_ref, vhi, vlo, xhi, xlo, out):
    both = nn(jnp.concatenate([xhi[...], xlo[...]], axis=0), vhi[...])
    change = both[:COLS] + both[COLS:] + nn(xhi[...], vlo[...])
    out[...] = c_ref[...] - change.T


def update(current, vhi, vlo, xhi, xlo):
    steps = ROWS // STEP
    return pl.pallas_call(
        update_kernel,
        grid=(steps,),
        in_specs=[
            pl.BlockSpec((STEP, COLS), lambda k: (k, 0)),
            pl.BlockSpec((NV, STEP), lambda k: (0, k)),
            pl.BlockSpec((NV, STEP), lambda k: (0, k)),
            pl.BlockSpec((COLS, NV), lambda k: (0, 0)),
            pl.BlockSpec((COLS, NV), lambda k: (0, 0)),
        ],
        out_specs=pl.BlockSpec((STEP, COLS), lambda k: (k, 0)),
        out_shape=jax.ShapeDtypeStruct((ROWS, COLS), F32),
        compiler_params=pltpu.CompilerParams(vmem_limit_bytes=VMEM),
        name="update",
    )(current, vhi, vlo, xhi, xlo)


def turn(chip, core):
    return 1 if (chip + core) % 2 == 0 else -1


def exchange(value, side):
    perm = []
    for chip in range(CHIPS):
        for core in range(2):
            target = (chip + side * turn(chip, core)) % CHIPS
            perm.append((chip * 2 + core, target * 2 + core))
    return lax.ppermute(value, "col", perm)


def swap_cores(value):
    return lax.ppermute(value, "col", [(i, i ^ 1) for i in range(2 * CHIPS)])


def shards(eigvecs, householder):
    me = lax.axis_index("col")
    chip, core = me // 2, me % 2
    sign = 1 - 2 * ((chip + core) % 2)
    steps = jnp.array(ARRIVAL, jnp.int32)
    here = ((chip + sign * steps + 8) % CHIPS) * 32 + core * 16
    there = ((chip - sign * steps + 8) % CHIPS) * 32 + (1 - core) * 16
    blocks = jnp.where(core == 0, jnp.array(GRAM_BLOCKS[0], jnp.int32), jnp.array(GRAM_BLOCKS[1], jnp.int32))
    place = jnp.concatenate([here, there, blocks.reshape(-1) * 128])

    own = householder.transpose(0, 2, 1).reshape(32, ROWS)
    first = exchange(own, 1)
    pieces = [jnp.concatenate([own, first], axis=0)]
    for side in (-1, 1, -1):
        pieces.append(exchange(pieces[-1], side))
    pieces += [swap_cores(piece) for piece in pieces]

    vhi, vlo, partial = products(place, pieces, eigvecs)
    summed = lax.all_to_all(partial, "row", 0, 0, tiled=True).sum(axis=0)
    mine = lax.all_to_all(jnp.broadcast_to(summed[None], (32, 40, COLS)), "row", 0, 0, tiled=True)
    other = swap_cores(mine[:, 16:, :])
    xhi, xlo = solve(core.reshape(1), mine, other)
    return update(eigvecs, vhi, vlo, xhi, xlo)


def solution(mesh):
    in_specs = (P("row", "col"), P(None, "row", "col"))
    out_specs = P("row", "col")
    return jax.shard_map(shards, mesh=mesh, in_specs=in_specs, out_specs=out_specs, check_vma=False)
```

```python
import jax
import jax.numpy as jnp
from jax import lax
from jax.experimental import pallas as pl
from jax.experimental.pallas import tpu as pltpu
from jax.sharding import PartitionSpec as P

F32 = jnp.float32
BF16 = jnp.bfloat16
CHIPS = 8
ROWS = 4096
COLS = 128
NV = 512
STEP = 1024
VMEM = 24 * 1024 * 1024
GRAM_BLOCKS = (
    ((0, 2), (0, 3), (1, 2), (1, 3)),
    ((0, 0), (0, 1), (1, 1), (2, 2), (2, 3), (3, 3)),
)


def split(value):
    high = value.astype(BF16)
    low = (value - high.astype(F32)).astype(BF16)
    return high, low


def nt(left, right):
    return lax.dot_general(left, right, (((1,), (1,)), ((), ())), preferred_element_type=F32)


def nn(left, right):
    return lax.dot_general(left, right, (((1,), (0,)), ((), ())), preferred_element_type=F32)


def hidot(left, right):
    return jnp.dot(left, right, precision=lax.Precision.HIGHEST, preferred_element_type=F32)


def assemble(place, pieces, vhi, vlo):
    for index, piece in enumerate(pieces):
        for block in range(2):
            high, low = split(piece[block * 16 : block * 16 + 16, :])
            at = pl.ds(pl.multiple_of(place[index] + block * 256, 16), 16)
            vhi[at, :] = high
            vlo[at, :] = low


def products_kernel(place, *refs):
    pieces = refs[:16]
    c_ref, out, proj, gram, vhi, vlo = refs[16:]
    step = pl.program_id(0)
    first_core = place[16] == 0

    @pl.when(step == 0)
    def _():
        proj[...] = jnp.zeros_like(proj)
        gram[...] = jnp.zeros_like(gram)

    assemble(place, pieces, vhi, vlo)
    chi, clo = split(c_ref[...])
    both = nn(vhi[...], jnp.concatenate([chi, clo], axis=1))
    proj[...] += both[:, :COLS] + both[:, COLS:] + nn(vlo[...], chi)

    @pl.when(first_core)
    def _():
        lhi, llo = vhi[:256, :], vlo[:256, :]
        rhi, rlo = vhi[256:, :], vlo[256:, :]
        gram[:256, :256] += nt(lhi, rhi) + nt(lhi, rlo) + nt(llo, rhi)

    @pl.when(jnp.logical_not(first_core))
    def _():
        for at in (0, 256):
            high, low = vhi[at : at + 256, :], vlo[at : at + 256, :]
            gram[at : at + 256, :256] += nt(high, high)
            gram[at : at + 256, 256:] += nt(high, low)

    @pl.when(step == pl.num_programs(0) - 1)
    def _():
        out[:, :16, :] = proj[...].reshape(32, 16, COLS)

        @pl.when(first_core)
        def _():
            cross = gram[:256, :256]
            parts = [cross[:128, :128], cross[:128, 128:], cross[128:, :128], cross[128:, 128:]]
            parts.append(jnp.zeros((256, 128), F32))
            out[:, 16:, :] = jnp.concatenate(parts, axis=0).reshape(32, 24, COLS)

        @pl.when(jnp.logical_not(first_core))
        def _():
            parts = []
            for at in (0, 256):
                mixed = gram[at : at + 256, 256:]
                square = gram[at : at + 256, :256] + mixed + mixed.T
                parts += [square[:128, :128], square[:128, 128:], square[128:, 128:]]
            out[:, 16:, :] = jnp.concatenate(parts, axis=0).reshape(32, 24, COLS)


def products(place, pieces, current):
    return pl.pallas_call(
        products_kernel,
        grid=(ROWS // STEP,),
        in_specs=[pl.BlockSpec(memory_space=pltpu.SMEM)]
        + [pl.BlockSpec((32, STEP), lambda k: (0, k))] * 16
        + [pl.BlockSpec((STEP, COLS), lambda k: (k, 0))],
        out_specs=pl.BlockSpec((32, 40, COLS), lambda k: (0, 0, 0)),
        out_shape=jax.ShapeDtypeStruct((32, 40, COLS), F32),
        scratch_shapes=[
            pltpu.VMEM((NV, COLS), F32),
            pltpu.VMEM((512, 512), F32),
            pltpu.VMEM((NV, STEP), BF16),
            pltpu.VMEM((NV, STEP), BF16),
        ],
        compiler_params=pltpu.CompilerParams(vmem_limit_bytes=VMEM),
        name="products",
    )(place, *pieces, current)


def invert_unit(nilpot):
    row = lax.broadcasted_iota(jnp.int32, (128, 128), 0)
    col = lax.broadcasted_iota(jnp.int32, (128, 128), 1)
    eye = (row == col).astype(F32)
    near = [jnp.where(row // 4 == col // 4, n, 0.0) for n in nilpot]
    square = [hidot(n, n) for n in near]
    inverse = [hidot(eye - n, eye + s) for n, s in zip(near, square)]
    size = 4
    while size < 128:
        pair = (row // (2 * size) == col // (2 * size)) & (row // size != col // size)
        right = [hidot(jnp.where(pair, n, 0.0), r) for n, r in zip(nilpot, inverse)]
        inverse = [r - hidot(r, t) for r, t in zip(inverse, right)]
        size *= 2
    return inverse


def solve_kernel(place, mine, other, xt):
    zero = place[16] == 0
    gram = {}
    for which in range(2):
        flat = jnp.where(zero == (which == 0), mine[:, 16:, :], other[...]).reshape(768, 128)
        for index, at in enumerate(GRAM_BLOCKS[which]):
            gram[at] = flat[index * 128 : index * 128 + 128]
    project = mine[:, :16, :].reshape(NV, COLS)
    row = lax.broadcasted_iota(jnp.int32, (128, 128), 0)
    col = lax.broadcasted_iota(jnp.int32, (128, 128), 1)
    scale = [2.0 / jnp.sum(jnp.where(row == col, gram[i, i], 0.0), axis=1, keepdims=True) for i in range(4)]
    inverse = invert_unit([jnp.where(row < col, gram[i, i] * scale[i], 0.0) for i in range(4)])
    coef = [None] * 4
    for i in range(3, -1, -1):
        rhs = project[i * 128 : i * 128 + 128]
        if i < 3:
            panel = jnp.concatenate([gram[i, j] for j in range(i + 1, 4)], axis=1)
            rhs = rhs - hidot(panel, jnp.concatenate(coef[i + 1 :], axis=0))
        coef[i] = hidot(inverse[i], rhs * scale[i])
    high, low = split(jnp.concatenate(coef, axis=0).T)
    xt[:COLS, :] = high
    xt[COLS:, :] = low


def solve(place, mine, other):
    return pl.pallas_call(
        solve_kernel,
        in_specs=[pl.BlockSpec(memory_space=pltpu.SMEM)] + [pl.BlockSpec(memory_space=pltpu.VMEM)] * 2,
        out_specs=pl.BlockSpec(memory_space=pltpu.VMEM),
        out_shape=jax.ShapeDtypeStruct((2 * COLS, NV), BF16),
        compiler_params=pltpu.CompilerParams(vmem_limit_bytes=VMEM),
        name="solve",
    )(place, mine, other)


def update_kernel(place, *refs):
    pieces = refs[:16]
    c_ref, xt, out, vhi, vlo = refs[16:]
    assemble(place, pieces, vhi, vlo)
    both = nn(xt[...], vhi[...])
    change = both[:COLS] + both[COLS:] + nn(xt[:COLS, :], vlo[...])
    out[...] = c_ref[...] - change.T


def update(place, pieces, current, xt):
    return pl.pallas_call(
        update_kernel,
        grid=(ROWS // STEP,),
        in_specs=[pl.BlockSpec(memory_space=pltpu.SMEM)]
        + [pl.BlockSpec((32, STEP), lambda k: (0, k))] * 16
        + [pl.BlockSpec((STEP, COLS), lambda k: (k, 0)), pl.BlockSpec((2 * COLS, NV), lambda k: (0, 0))],
        out_specs=pl.BlockSpec((STEP, COLS), lambda k: (k, 0)),
        out_shape=jax.ShapeDtypeStruct((ROWS, COLS), F32),
        scratch_shapes=[pltpu.VMEM((NV, STEP), BF16), pltpu.VMEM((NV, STEP), BF16)],
        compiler_params=pltpu.CompilerParams(vmem_limit_bytes=VMEM),
        name="update",
    )(place, *pieces, current, xt)


def shift(value, way):
    perm = []
    for chip in range(CHIPS):
        for core in range(2):
            target = (chip + way * (1 - 2 * core)) % CHIPS
            perm.append((chip * 2 + core, target * 2 + core))
    return lax.ppermute(value, "col", perm)


def swap_cores(value):
    return lax.ppermute(value, "col", [(i, i ^ 1) for i in range(2 * CHIPS)])


def shards(eigvecs, householder):
    me = lax.axis_index("col")
    chip, core = me // 2, me % 2
    steps = jnp.array((0, -1, 1, -2, 2, -3, 3, -4), jnp.int32) * (1 - 2 * core)
    here = ((chip + steps + 8) % CHIPS) * 32 + core * 16
    there = ((chip - steps + 8) % CHIPS) * 32 + (1 - core) * 16
    place = jnp.concatenate([here, there, core.reshape(1)])

    own = householder.transpose(0, 2, 1).reshape(32, ROWS)
    pieces = [own]
    ahead = behind = own
    for _ in range(3):
        ahead, behind = shift(ahead, 1), shift(behind, -1)
        pieces += [ahead, behind]
    pieces.append(shift(ahead, 1))
    pieces += [swap_cores(piece) for piece in pieces]

    partial = products(place, pieces, eigvecs)
    summed = lax.all_to_all(partial, "row", 0, 0, tiled=True).sum(axis=0)
    mine = lax.all_to_all(jnp.broadcast_to(summed[None], (32, 40, COLS)), "row", 0, 0, tiled=True)
    other = swap_cores(mine[:, 16:, :])
    return update(place, pieces, eigvecs, solve(place, mine, other))


def solution(mesh):
    in_specs = (P("row", "col"), P(None, "row", "col"))
    out_specs = P("row", "col")
    return jax.shard_map(shards, mesh=mesh, in_specs=in_specs, out_specs=out_specs, check_vma=False)
```

```python
import jax
import jax.numpy as jnp
from jax import lax
from jax.experimental import pallas as pl
from jax.experimental.pallas import tpu as pltpu
from jax.sharding import PartitionSpec as P

F32 = jnp.float32
BF16 = jnp.bfloat16
CHIPS = 8
ROWS = 4096
COLS = 128
NV = 512
STEP = 1024
VMEM = 24 * 1024 * 1024
GRAM_BLOCKS = (
    ((0, 2), (0, 3), (1, 2), (1, 3)),
    ((0, 0), (0, 1), (1, 1), (2, 2), (2, 3), (3, 3)),
)


def split(value):
    high = value.astype(BF16)
    low = (value - high.astype(F32)).astype(BF16)
    return high, low


def nt(left, right):
    return lax.dot_general(left, right, (((1,), (1,)), ((), ())), preferred_element_type=F32)


def nn(left, right):
    return lax.dot_general(left, right, (((1,), (0,)), ((), ())), preferred_element_type=F32)


def hidot(left, right):
    return jnp.dot(left, right, precision=lax.Precision.HIGHEST, preferred_element_type=F32)


def assemble(place, pieces, vhi, vlo):
    index = 0
    for piece in pieces:
        for first in range(0, piece.shape[0], 16):
            high, low = split(piece[first : first + 16, :])
            at = pl.ds(pl.multiple_of(place[index], 16), 16)
            vhi[at, :] = high
            vlo[at, :] = low
            index += 1


def add_projection(proj, c_ref, vhi, vlo):
    chi, clo = split(c_ref[...])
    both = nn(vhi[...], jnp.concatenate([chi, clo], axis=1))
    proj[...] += both[:, :COLS] + both[:, COLS:] + nn(vlo[...], chi)


def add_square(gram, vhi, vlo):
    gram[:, :256] += nt(vhi[...], vhi[...])
    gram[:, 256:] += nt(vhi[...], vlo[...])


def upper_blocks(gram):
    mixed = gram[:, 256:]
    square = gram[:, :256] + mixed + mixed.T
    return [square[:128, :128], square[:128, 128:], square[128:, 128:]]


def later_kernel(place, *refs):
    pieces = refs[:8]
    c_ref, vhi, vlo, proj, out, gram = refs[8:]
    step = pl.program_id(0)

    @pl.when(step == 0)
    def _():
        proj[...] = jnp.zeros_like(proj)
        gram[...] = jnp.zeros_like(gram)

    assemble(place, pieces, vhi, vlo)
    add_projection(proj, c_ref, vhi, vlo)

    @pl.when(place[16] == 1)
    def _():
        add_square(gram, vhi, vlo)

    @pl.when(step == pl.num_programs(0) - 1)
    def _():
        out[...] = jnp.concatenate(upper_blocks(gram), axis=0)


def strip(rows):
    return pl.BlockSpec((rows, STEP), lambda k: (0, k))


def whole(*shape):
    return pl.BlockSpec(shape, lambda k: (0,) * len(shape))


def later_products(place, pieces, current):
    return pl.pallas_call(
        later_kernel,
        grid=(ROWS // STEP,),
        in_specs=[pl.BlockSpec(memory_space=pltpu.SMEM)]
        + [strip(piece.shape[0]) for piece in pieces]
        + [pl.BlockSpec((STEP, COLS), lambda k: (k, 0))],
        out_specs=[strip(256), strip(256), whole(256, COLS), whole(384, 128)],
        out_shape=[
            jax.ShapeDtypeStruct((256, ROWS), BF16),
            jax.ShapeDtypeStruct((256, ROWS), BF16),
            jax.ShapeDtypeStruct((256, COLS), F32),
            jax.ShapeDtypeStruct((384, 128), F32),
        ],
        scratch_shapes=[pltpu.VMEM((256, 512), F32)],
        compiler_params=pltpu.CompilerParams(vmem_limit_bytes=VMEM),
        cost_estimate=pl.CostEstimate(flops=4 * 10**9, bytes_accessed=10 * 2**20, transcendentals=0),
        name="later_products",
    )(place, *pieces, current)


def earlier_kernel(place, mine, other, c_ref, whi, wlo, proj1, gram1, vhi, vlo, out, proj, gram):
    step = pl.program_id(0)
    first_core = place[16] == 0

    @pl.when(step == 0)
    def _():
        proj[...] = jnp.zeros_like(proj)
        gram[...] = jnp.zeros_like(gram)

    assemble(place, [mine, other], vhi, vlo)
    add_projection(proj, c_ref, vhi, vlo)

    @pl.when(first_core)
    def _():
        gram[:, :256] += nt(vhi[...], whi[...]) + nt(vhi[...], wlo[...]) + nt(vlo[...], whi[...])

    @pl.when(jnp.logical_not(first_core))
    def _():
        add_square(gram, vhi, vlo)

    @pl.when(step == pl.num_programs(0) - 1)
    def _():
        out[:, :16, :] = jnp.concatenate([proj[...], proj1[...]], axis=0).reshape(32, 16, COLS)

        @pl.when(first_core)
        def _():
            cross = gram[:, :256]
            parts = [cross[:128, :128], cross[:128, 128:], cross[128:, :128], cross[128:, 128:]]
            parts.append(jnp.zeros((256, 128), F32))
            out[:, 16:, :] = jnp.concatenate(parts, axis=0).reshape(32, 24, COLS)

        @pl.when(jnp.logical_not(first_core))
        def _():
            parts = upper_blocks(gram) + [gram1[...]]
            out[:, 16:, :] = jnp.concatenate(parts, axis=0).reshape(32, 24, COLS)


def earlier_products(place, mine, other, current, later):
    whi, wlo, proj1, gram1 = later
    return pl.pallas_call(
        earlier_kernel,
        grid=(ROWS // STEP,),
        in_specs=[
            pl.BlockSpec(memory_space=pltpu.SMEM),
            strip(128),
            strip(128),
            pl.BlockSpec((STEP, COLS), lambda k: (k, 0)),
            strip(256),
            strip(256),
            whole(256, COLS),
            whole(384, 128),
        ],
        out_specs=[strip(256), strip(256), whole(32, 40, COLS)],
        out_shape=[
            jax.ShapeDtypeStruct((256, ROWS), BF16),
            jax.ShapeDtypeStruct((256, ROWS), BF16),
            jax.ShapeDtypeStruct((32, 40, COLS), F32),
        ],
        scratch_shapes=[pltpu.VMEM((256, COLS), F32), pltpu.VMEM((256, 512), F32)],
        compiler_params=pltpu.CompilerParams(vmem_limit_bytes=VMEM),
        cost_estimate=pl.CostEstimate(flops=4 * 10**9, bytes_accessed=14 * 2**20, transcendentals=0),
        name="earlier_products",
    )(place, mine, other, current, whi, wlo, proj1, gram1)


def invert_unit(nilpot):
    row = lax.broadcasted_iota(jnp.int32, (128, 128), 0)
    col = lax.broadcasted_iota(jnp.int32, (128, 128), 1)
    eye = (row == col).astype(F32)
    near = [jnp.where(row // 4 == col // 4, n, 0.0) for n in nilpot]
    square = [hidot(n, n) for n in near]
    inverse = [hidot(eye - n, eye + s) for n, s in zip(near, square)]
    size = 4
    while size < 128:
        pair = (row // (2 * size) == col // (2 * size)) & (row // size != col // size)
        right = [hidot(jnp.where(pair, n, 0.0), r) for n, r in zip(nilpot, inverse)]
        inverse = [r - hidot(r, t) for r, t in zip(inverse, right)]
        size *= 2
    return inverse


def solve_kernel(place, mine, other, xt):
    zero = place[16] == 0
    gram = {}
    for which in range(2):
        flat = jnp.where(zero == (which == 0), mine[:, 16:, :], other[...]).reshape(768, 128)
        for index, at in enumerate(GRAM_BLOCKS[which]):
            gram[at] = flat[index * 128 : index * 128 + 128]
    project = mine[:, :16, :].reshape(NV, COLS)
    row = lax.broadcasted_iota(jnp.int32, (128, 128), 0)
    col = lax.broadcasted_iota(jnp.int32, (128, 128), 1)
    scale = [2.0 / jnp.sum(jnp.where(row == col, gram[i, i], 0.0), axis=1, keepdims=True) for i in range(4)]
    inverse = invert_unit([jnp.where(row < col, gram[i, i] * scale[i], 0.0) for i in range(4)])
    coef = [None] * 4
    for i in range(3, -1, -1):
        rhs = project[i * 128 : i * 128 + 128]
        if i < 3:
            panel = jnp.concatenate([gram[i, j] for j in range(i + 1, 4)], axis=1)
            rhs = rhs - hidot(panel, jnp.concatenate(coef[i + 1 :], axis=0))
        coef[i] = hidot(inverse[i], rhs * scale[i])
    high, low = split(jnp.concatenate(coef, axis=0).T)
    xt[:COLS, :] = high
    xt[COLS:, :] = low


def solve(place, mine, other):
    return pl.pallas_call(
        solve_kernel,
        in_specs=[pl.BlockSpec(memory_space=pltpu.SMEM)] + [pl.BlockSpec(memory_space=pltpu.VMEM)] * 2,
        out_specs=pl.BlockSpec(memory_space=pltpu.VMEM),
        out_shape=jax.ShapeDtypeStruct((2 * COLS, NV), BF16),
        compiler_params=pltpu.CompilerParams(vmem_limit_bytes=VMEM),
        name="solve",
    )(place, mine, other)


def update_kernel(c_ref, vhi, vlo, whi, wlo, xt, out):
    xhi = xt[:COLS, :]
    change = nn(xhi[:, :256], vlo[...]) + nn(xhi[:, 256:], wlo[...])
    both = nn(xt[:, :256], vhi[...]) + nn(xt[:, 256:], whi[...])
    out[...] = c_ref[...] - (change + both[:COLS] + both[COLS:]).T


def update(current, parts, xt):
    return pl.pallas_call(
        update_kernel,
        grid=(ROWS // STEP,),
        in_specs=[pl.BlockSpec((STEP, COLS), lambda k: (k, 0))] + [strip(256)] * 4 + [whole(2 * COLS, NV)],
        out_specs=pl.BlockSpec((STEP, COLS), lambda k: (k, 0)),
        out_shape=jax.ShapeDtypeStruct((ROWS, COLS), F32),
        compiler_params=pltpu.CompilerParams(vmem_limit_bytes=VMEM),
        name="update",
    )(current, *parts, xt)


def shift(value, way):
    perm = []
    for chip in range(CHIPS):
        for core in range(2):
            target = (chip + way * (1 - 2 * core)) % CHIPS
            perm.append((chip * 2 + core, target * 2 + core))
    return lax.ppermute(value, "col", perm)


def swap_cores(value):
    return lax.ppermute(value, "col", [(i, i ^ 1) for i in range(2 * CHIPS)])


def shards(eigvecs, householder):
    me = lax.axis_index("col")
    chip, core = me // 2, me % 2
    steps = jnp.array((0, -1, 1, -2, 2, -3, 3, -4), jnp.int32) * (1 - 2 * core)
    here = ((chip + steps + 8) % CHIPS) * 32 + core * 16
    there = ((chip - steps + 8) % CHIPS) * 32 + (1 - core) * 16
    later_place = jnp.concatenate([here, there, core.reshape(1)])
    order = jnp.arange(CHIPS, dtype=jnp.int32) * 32
    earlier_place = jnp.concatenate([order + core * 16, order + (1 - core) * 16, core.reshape(1)])

    own = householder.transpose(0, 2, 1)
    same_core = [[2 * chip + core for chip in range(CHIPS)] for core in range(2)]
    mine = lax.all_gather(own[0], "col", axis=0, tiled=True, axis_index_groups=same_core)

    ahead = behind = own[1]
    groups = [[own[1]]]
    for step in range(3):
        ahead, behind = shift(ahead, 1), shift(behind, -1)
        if step:
            groups.append([])
        groups[-1] += [ahead, behind]
    mine, last, groups[-1][1] = lax.optimization_barrier((mine, shift(ahead, 1), behind))
    pieces = [jnp.concatenate(group, axis=0) for group in groups] + [last]
    pieces += [swap_cores(piece) for piece in pieces]
    later = later_products(later_place, pieces, eigvecs)
    vhi, vlo, partial = earlier_products(earlier_place, mine, swap_cores(mine), eigvecs, later)

    summed = lax.all_to_all(partial, "row", 0, 0, tiled=True).sum(axis=0)
    total = lax.all_to_all(jnp.broadcast_to(summed[None], (32, 40, COLS)), "row", 0, 0, tiled=True)
    coef = solve(earlier_place, total, swap_cores(total[:, 16:, :]))
    return update(eigvecs, (vhi, vlo, later[0], later[1]), coef)


def solution(mesh):
    in_specs = (P("row", "col"), P(None, "row", "col"))
    out_specs = P("row", "col")
    return jax.shard_map(shards, mesh=mesh, in_specs=in_specs, out_specs=out_specs, check_vma=False)
```

```python
import jax
import jax.numpy as jnp
from jax import lax
from jax.experimental import pallas as pl
from jax.experimental.pallas import tpu as pltpu
from jax.sharding import PartitionSpec as P

F32 = jnp.float32
BF16 = jnp.bfloat16
CHIPS = 8
ROWS = 4096
COLS = 128
NV = 512
STEP = 1024
VMEM = 24 * 1024 * 1024
MOST_VMEM = 56 * 1024 * 1024
ARRIVAL = ((0, 1), (-1, -2), (2, 3), (-3, -4))
GRAM_BLOCKS = (
    ((0, 2), (0, 3), (1, 2), (1, 3)),
    ((0, 0), (0, 1), (1, 1), (2, 2), (2, 3), (3, 3)),
)


def split(value):
    high = value.astype(BF16)
    low = (value - high.astype(F32)).astype(BF16)
    return high, low


def nt(left, right):
    return lax.dot_general(left, right, (((1,), (1,)), ((), ())), preferred_element_type=F32)


def nn(left, right):
    return lax.dot_general(left, right, (((1,), (0,)), ((), ())), preferred_element_type=F32)


def hidot(left, right):
    return jnp.dot(left, right, precision=lax.Precision.HIGHEST, preferred_element_type=F32)


def assemble(me, pieces, vhi, vlo):
    chip, core = me // 2, me % 2
    turn = 1 - 2 * ((chip + core) % 2)
    for index, piece in enumerate(pieces):
        swapped, arrival, block = index // 8, index % 8 // 2, index % 2
        for half in range(2):
            step = ARRIVAL[arrival][half] * (1 - 2 * swapped)
            source = (chip + turn * step + CHIPS) % CHIPS
            column = block * 256 + source * 32 + (1 - core if swapped else core) * 16
            high, low = split(piece[half * 16 : half * 16 + 16, :])
            at = pl.ds(pl.multiple_of(column, 16), 16)
            vhi[at, :] = high
            vlo[at, :] = low


def strip(rows):
    return pl.BlockSpec((rows, STEP), lambda k: (0, k))


def whole(*shape):
    return pl.BlockSpec(shape, lambda k: (0,) * len(shape))


def products_kernel(me, *refs):
    pieces = refs[:16]
    c_ref, vhi, vlo, out, proj, gram = refs[16:]
    step = pl.program_id(0)
    first_core = me[0] % 2 == 0

    @pl.when(step == 0)
    def _():
        proj[...] = jnp.zeros_like(proj)
        gram[...] = jnp.zeros_like(gram)

    assemble(me[0], pieces, vhi, vlo)
    chi, clo = split(c_ref[...])
    both = nn(vhi[...], jnp.concatenate([chi, clo], axis=1))
    proj[...] += both[:, :COLS] + both[:, COLS:] + nn(vlo[...], chi)

    @pl.when(first_core)
    def _():
        lhi, llo = vhi[:256, :], vlo[:256, :]
        rhi, rlo = vhi[256:, :], vlo[256:, :]
        gram[:256, :256] += nt(lhi, rhi) + nt(lhi, rlo) + nt(llo, rhi)

    @pl.when(jnp.logical_not(first_core))
    def _():
        for at in (0, 256):
            high, low = vhi[at : at + 256, :], vlo[at : at + 256, :]
            gram[at : at + 256, :256] += nt(high, high)
            gram[at : at + 256, 256:] += nt(high, low)

    @pl.when(step == pl.num_programs(0) - 1)
    def _():
        out[:, :16, :] = proj[...].reshape(32, 16, COLS)

        @pl.when(first_core)
        def _():
            cross = gram[:256, :256]
            parts = [cross[:128, :128], cross[:128, 128:], cross[128:, :128], cross[128:, 128:]]
            parts.append(jnp.zeros((256, 128), F32))
            out[:, 16:, :] = jnp.concatenate(parts, axis=0).reshape(32, 24, COLS)

        @pl.when(jnp.logical_not(first_core))
        def _():
            parts = []
            for at in (0, 256):
                mixed = gram[at : at + 256, 256:]
                square = gram[at : at + 256, :256] + mixed + mixed.T
                parts += [square[:128, :128], square[:128, 128:], square[128:, 128:]]
            out[:, 16:, :] = jnp.concatenate(parts, axis=0).reshape(32, 24, COLS)


def products(me, pieces, current):
    return pl.pallas_call(
        products_kernel,
        grid=(ROWS // STEP,),
        in_specs=[pl.BlockSpec(memory_space=pltpu.SMEM)]
        + [strip(32)] * 16
        + [pl.BlockSpec((STEP, COLS), lambda k: (k, 0))],
        out_specs=[strip(NV), strip(NV), whole(32, 40, COLS)],
        out_shape=[
            pltpu.HBM((NV, ROWS), BF16),
            pltpu.HBM((NV, ROWS), BF16),
            jax.ShapeDtypeStruct((32, 40, COLS), F32),
        ],
        scratch_shapes=[pltpu.VMEM((NV, COLS), F32), pltpu.VMEM((512, 512), F32)],
        compiler_params=pltpu.CompilerParams(vmem_limit_bytes=VMEM),
        name="products",
    )(me, *pieces, current)


def invert_unit(nilpot):
    row = lax.broadcasted_iota(jnp.int32, (128, 128), 0)
    col = lax.broadcasted_iota(jnp.int32, (128, 128), 1)
    eye = (row == col).astype(F32)
    near = [jnp.where(row // 4 == col // 4, n, 0.0) for n in nilpot]
    square = [hidot(n, n) for n in near]
    inverse = [hidot(eye - n, eye + s) for n, s in zip(near, square)]
    size = 4
    while size < 128:
        pair = (row // (2 * size) == col // (2 * size)) & (row // size != col // size)
        right = [hidot(jnp.where(pair, n, 0.0), r) for n, r in zip(nilpot, inverse)]
        inverse = [r - hidot(r, t) for r, t in zip(inverse, right)]
        size *= 2
    return inverse


def solve_kernel(me, mine, other, xt):
    zero = me[0] % 2 == 0
    gram = {}
    for which in range(2):
        flat = jnp.where(zero == (which == 0), mine[:, 16:, :], other[...]).reshape(768, 128)
        for index, at in enumerate(GRAM_BLOCKS[which]):
            gram[at] = flat[index * 128 : index * 128 + 128]
    project = mine[:, :16, :].reshape(NV, COLS)
    row = lax.broadcasted_iota(jnp.int32, (128, 128), 0)
    col = lax.broadcasted_iota(jnp.int32, (128, 128), 1)
    scale = [2.0 / jnp.sum(jnp.where(row == col, gram[i, i], 0.0), axis=1, keepdims=True) for i in range(4)]
    inverse = invert_unit([jnp.where(row < col, gram[i, i] * scale[i], 0.0) for i in range(4)])
    coef = [None] * 4
    for i in range(3, -1, -1):
        rhs = project[i * 128 : i * 128 + 128]
        if i < 3:
            panel = jnp.concatenate([gram[i, j] for j in range(i + 1, 4)], axis=1)
            rhs = rhs - hidot(panel, jnp.concatenate(coef[i + 1 :], axis=0))
        coef[i] = hidot(inverse[i], rhs * scale[i])
    high, low = split(jnp.concatenate(coef, axis=0).T)
    xt[:COLS, :] = high
    xt[COLS:, :] = low


def solve(me, mine, other):
    return pl.pallas_call(
        solve_kernel,
        in_specs=[pl.BlockSpec(memory_space=pltpu.SMEM)] + [pl.BlockSpec(memory_space=pltpu.VMEM)] * 2,
        out_specs=pl.BlockSpec(memory_space=pltpu.VMEM),
        out_shape=pltpu.HBM((2 * COLS, NV), BF16),
        compiler_params=pltpu.CompilerParams(vmem_limit_bytes=VMEM),
        name="solve",
    )(me, mine, other)


def update_kernel(c_ref, vhi, vlo, xt, out):
    both = nn(xt[...], vhi[...])
    change = both[:COLS] + both[COLS:] + nn(xt[:COLS, :], vlo[...])
    out[...] = c_ref[...] - change.T


def update(current, vhi, vlo, xt):
    return pl.pallas_call(
        update_kernel,
        grid=(ROWS // STEP,),
        in_specs=[pl.BlockSpec((STEP, COLS), lambda k: (k, 0)), strip(NV), strip(NV), whole(2 * COLS, NV)],
        out_specs=pl.BlockSpec((STEP, COLS), lambda k: (k, 0)),
        out_shape=jax.ShapeDtypeStruct((ROWS, COLS), F32),
        compiler_params=pltpu.CompilerParams(vmem_limit_bytes=MOST_VMEM),
        name="update",
    )(current, vhi, vlo, xt)


def exchange(value, side):
    perm = []
    for chip in range(CHIPS):
        for core in range(2):
            turn = 1 if (chip + core) % 2 == 0 else -1
            target = (chip + side * turn) % CHIPS
            perm.append((chip * 2 + core, target * 2 + core))
    return lax.ppermute(value, "col", perm)


def swap_cores(value):
    return lax.ppermute(value, "col", [(i, i ^ 1) for i in range(2 * CHIPS)])


def shards(eigvecs, householder):
    me = lax.axis_index("col").reshape(1)
    own = householder.transpose(0, 2, 1)
    chains = [own[0], own[1]]
    chains = [jnp.concatenate([piece, exchange(piece, 1)], axis=0) for piece in chains]
    pieces = list(chains)
    for side in (-1, 1, -1):
        chains = [exchange(piece, side) for piece in chains]
        pieces += chains
    pieces += [swap_cores(piece) for piece in pieces]

    vhi, vlo, partial = products(me, pieces, eigvecs)
    summed = lax.all_to_all(partial, "row", 0, 0, tiled=True).sum(axis=0)
    mine = lax.all_to_all(jnp.broadcast_to(summed[None], (32, 40, COLS)), "row", 0, 0, tiled=True)
    other = swap_cores(mine[:, 16:, :])
    return update(eigvecs, vhi, vlo, solve(me, mine, other))


def solution(mesh):
    in_specs = (P("row", "col"), P(None, "row", "col"))
    out_specs = P("row", "col")
    return jax.shard_map(shards, mesh=mesh, in_specs=in_specs, out_specs=out_specs, check_vma=False)
```

```python
import jax
import jax.numpy as jnp
from jax import lax
from jax.experimental import pallas as pl
from jax.experimental.pallas import tpu as pltpu
from jax.sharding import PartitionSpec as P

F32 = jnp.float32
BF16 = jnp.bfloat16
CHIPS = 8
ROWS = 4096
COLS = 128
NV = 512
PARTS = tuple(pl.ds(first, 1024) for first in range(0, ROWS, 1024))
VMEM = 32 * 1024 * 1024
ARRIVAL = ((0, 1), (-1, -2), (2, 3), (-3, -4))
GRAM_BLOCKS = (
    ((0, 2), (0, 3), (1, 2), (1, 3)),
    ((0, 0), (0, 1), (1, 1), (2, 2), (2, 3), (3, 3)),
)


def split(value):
    high = value.astype(BF16)
    low = (value - high.astype(F32)).astype(BF16)
    return high, low


def nt(left, right):
    return lax.dot_general(left, right, (((1,), (1,)), ((), ())), preferred_element_type=F32)


def nn(left, right):
    return lax.dot_general(left, right, (((1,), (0,)), ((), ())), preferred_element_type=F32)


def hidot(left, right):
    return jnp.dot(left, right, precision=lax.Precision.HIGHEST, preferred_element_type=F32)


def assemble(me, index, piece, vhi, vlo):
    chip, core = me // 2, me % 2
    turn = 1 - 2 * ((chip + core) % 2)
    swapped, arrival, block = index // 8, index % 8 // 2, index % 2
    for half in range(2):
        step = ARRIVAL[arrival][half] * (1 - 2 * swapped)
        source = (chip + turn * step + CHIPS) % CHIPS
        column = block * 256 + source * 32 + (1 - core if swapped else core) * 16
        high, low = split(piece[half * 16 : half * 16 + 16, :])
        at = pl.ds(pl.multiple_of(column, 16), 16)
        vhi[at, :] = high
        vlo[at, :] = low


def products_kernel(me, *refs):
    pieces = refs[:16]
    c_hbm, vhi_hbm, vlo_hbm, out, raw, c_ref, vhi, vlo, come, gone = refs[16:]
    first_core = me[0] % 2 == 0
    incoming = [pltpu.make_async_copy(piece, raw.at[n], come.at[n]) for n, piece in enumerate(pieces)]
    for index, at in enumerate(PARTS):
        incoming.append(pltpu.make_async_copy(c_hbm.at[at], c_ref.at[at], come.at[16 + index]))
    for copy in incoming:
        copy.start()
    for n in sorted(range(16), key=lambda n: -(n % 8)):
        incoming[n].wait()
        assemble(me[0], n, raw.at[n], vhi, vlo)
    outgoing = []
    for index, at in enumerate(PARTS):
        for which, (here, there) in enumerate(((vhi, vhi_hbm), (vlo, vlo_hbm))):
            outgoing.append(pltpu.make_async_copy(here.at[:, at], there.at[:, at], gone.at[index, which]))
            outgoing[-1].start()
    for copy in incoming[16:]:
        copy.wait()
    chi, clo = split(c_ref[...])
    both = nn(vhi[...], jnp.concatenate([chi, clo], axis=1))
    proj = both[:, :COLS] + both[:, COLS:] + nn(vlo[...], chi)
    out[:, :16, :] = proj.reshape(32, 16, COLS)

    @pl.when(first_core)
    def _():
        cross = nt(vhi[:256, :], vhi[256:, :]) + nt(vhi[:256, :], vlo[256:, :]) + nt(vlo[:256, :], vhi[256:, :])
        parts = [cross[:128, :128], cross[:128, 128:], cross[128:, :128], cross[128:, 128:]]
        parts.append(jnp.zeros((256, 128), F32))
        out[:, 16:, :] = jnp.concatenate(parts, axis=0).reshape(32, 24, COLS)

    @pl.when(jnp.logical_not(first_core))
    def _():
        parts = []
        for at in (0, 256):
            high = vhi[at : at + 256, :]
            mixed = nt(high, vlo[at : at + 256, :])
            square = nt(high, high) + mixed + mixed.T
            parts += [square[:128, :128], square[:128, 128:], square[128:, 128:]]
        out[:, 16:, :] = jnp.concatenate(parts, axis=0).reshape(32, 24, COLS)

    for copy in outgoing:
        copy.wait()


def products(me, pieces, current):
    return pl.pallas_call(
        products_kernel,
        in_specs=[pl.BlockSpec(memory_space=pltpu.SMEM)] + [pl.BlockSpec(memory_space=pl.ANY)] * 17,
        out_specs=[pl.BlockSpec(memory_space=pl.ANY)] * 2 + [pl.BlockSpec(memory_space=pltpu.VMEM)],
        out_shape=[
            pltpu.HBM((NV, ROWS), BF16),
            pltpu.HBM((NV, ROWS), BF16),
            jax.ShapeDtypeStruct((32, 40, COLS), F32),
        ],
        scratch_shapes=[
            pltpu.VMEM((16, 32, ROWS), F32),
            pltpu.VMEM((ROWS, COLS), F32),
            pltpu.VMEM((NV, ROWS), BF16),
            pltpu.VMEM((NV, ROWS), BF16),
            pltpu.SemaphoreType.DMA((16 + len(PARTS),)),
            pltpu.SemaphoreType.DMA((len(PARTS), 2)),
        ],
        compiler_params=pltpu.CompilerParams(vmem_limit_bytes=VMEM),
        name="products",
    )(me, *pieces, current)


def invert_unit(nilpot):
    row = lax.broadcasted_iota(jnp.int32, (128, 128), 0)
    col = lax.broadcasted_iota(jnp.int32, (128, 128), 1)
    eye = (row == col).astype(F32)
    near = [jnp.where(row // 4 == col // 4, n, 0.0) for n in nilpot]
    square = [hidot(n, n) for n in near]
    inverse = [hidot(eye - n, eye + s) for n, s in zip(near, square)]
    size = 4
    while size < 128:
        pair = (row // (2 * size) == col // (2 * size)) & (row // size != col // size)
        right = [hidot(jnp.where(pair, n, 0.0), r) for n, r in zip(nilpot, inverse)]
        inverse = [r - hidot(r, t) for r, t in zip(inverse, right)]
        size *= 2
    return inverse


def coefficients(me, mine, other):
    zero = me[0] % 2 == 0
    gram = {}
    for which in range(2):
        flat = jnp.where(zero == (which == 0), mine[:, 16:, :], other[...]).reshape(768, 128)
        for index, at in enumerate(GRAM_BLOCKS[which]):
            gram[at] = flat[index * 128 : index * 128 + 128]
    project = mine[:, :16, :].reshape(NV, COLS)
    row = lax.broadcasted_iota(jnp.int32, (128, 128), 0)
    col = lax.broadcasted_iota(jnp.int32, (128, 128), 1)
    scale = [2.0 / jnp.sum(jnp.where(row == col, gram[i, i], 0.0), axis=1, keepdims=True) for i in range(4)]
    inverse = invert_unit([jnp.where(row < col, gram[i, i] * scale[i], 0.0) for i in range(4)])
    wide = []
    for i in (0, 2):
        corner = hidot(inverse[i], hidot(gram[i, i + 1] * scale[i], inverse[i + 1]))
        upper = jnp.concatenate([inverse[i], -corner], axis=1)
        lower = jnp.concatenate([jnp.zeros((128, 128), F32), inverse[i + 1]], axis=1)
        wide.append(jnp.concatenate([upper, lower], axis=0))
    scales = [jnp.concatenate(scale[i : i + 2], axis=0) for i in (0, 2)]
    cross = jnp.concatenate([jnp.concatenate([gram[i, 2], gram[i, 3]], axis=1) for i in (0, 1)], axis=0)
    later = hidot(wide[1], project[256:] * scales[1])
    coef = [hidot(wide[0], (project[:256] - hidot(cross, later)) * scales[0]), later]
    return split(jnp.concatenate(coef, axis=0).T)


def finish_kernel(me, mine, other, c_hbm, vhi_hbm, vlo_hbm, out, c_ref, vhi, vlo, done, come, gone):
    copies = []
    for index, at in enumerate(PARTS):
        pairs = ((vhi_hbm.at[:, at], vhi.at[:, at]), (vlo_hbm.at[:, at], vlo.at[:, at]), (c_hbm.at[at], c_ref.at[at]))
        copies.append([pltpu.make_async_copy(*pair, come.at[index, which]) for which, pair in enumerate(pairs)])
        for copy in copies[-1]:
            copy.start()
    xhi, xlo = coefficients(me, mine, other)
    both = jnp.concatenate([xhi, xlo], axis=0)
    writes = []
    for index in range(0, len(PARTS), 2):
        for copy in copies[index] + copies[index + 1]:
            copy.wait()
        rows = pl.ds(PARTS[index].start, PARTS[index].size * 2)
        first = nn(both, vhi[:, rows])
        change = first[:COLS] + first[COLS:] + nn(xhi, vlo[:, rows])
        for half, at in enumerate(PARTS[index : index + 2]):
            done[at, :] = c_ref[at, :] - change[:, half * at.size : (half + 1) * at.size].T
            writes.append(pltpu.make_async_copy(done.at[at], out.at[at], gone.at[index + half]))
            writes[-1].start()
    for write in writes:
        write.wait()


def finish(me, mine, other, current, vhi, vlo):
    return pl.pallas_call(
        finish_kernel,
        in_specs=[pl.BlockSpec(memory_space=pltpu.SMEM)]
        + [pl.BlockSpec(memory_space=pltpu.VMEM)] * 2
        + [pl.BlockSpec(memory_space=pl.ANY)] * 3,
        out_specs=pl.BlockSpec(memory_space=pl.ANY),
        out_shape=jax.ShapeDtypeStruct((ROWS, COLS), F32),
        scratch_shapes=[
            pltpu.VMEM((ROWS, COLS), F32),
            pltpu.VMEM((NV, ROWS), BF16),
            pltpu.VMEM((NV, ROWS), BF16),
            pltpu.VMEM((ROWS, COLS), F32),
            pltpu.SemaphoreType.DMA((len(PARTS), 3)),
            pltpu.SemaphoreType.DMA((len(PARTS),)),
        ],
        compiler_params=pltpu.CompilerParams(vmem_limit_bytes=VMEM),
        name="finish",
    )(me, mine, other, current, vhi, vlo)


def exchange(value, side):
    perm = []
    for chip in range(CHIPS):
        for core in range(2):
            turn = 1 if (chip + core) % 2 == 0 else -1
            target = (chip + side * turn) % CHIPS
            perm.append((chip * 2 + core, target * 2 + core))
    return lax.ppermute(value, "col", perm)


def in_hbm(value):
    return pltpu.with_memory_space_constraint(value, pltpu.HBM)


def swap_cores(value):
    return lax.ppermute(value, "col", [(i, i ^ 1) for i in range(2 * CHIPS)])


def shards(eigvecs, householder):
    me = lax.axis_index("col").reshape(1)
    own = householder.transpose(0, 2, 1)
    chains = [own[0], own[1]]
    chains = [jnp.concatenate([piece, exchange(piece, 1)], axis=0) for piece in chains]
    pieces = list(chains)
    for side in (-1, 1, -1):
        chains = [exchange(piece, side) for piece in chains]
        pieces += chains
    pieces += [swap_cores(piece) for piece in pieces]

    vhi, vlo, partial = products(me, [in_hbm(piece) if n % 8 < 4 else piece for n, piece in enumerate(pieces)], in_hbm(eigvecs))
    summed = lax.all_to_all(partial, "row", 0, 0, tiled=True).sum(axis=0)
    mine = lax.all_to_all(jnp.broadcast_to(summed[None], (32, 40, COLS)), "row", 0, 0, tiled=True)
    other = swap_cores(mine[:, 16:, :])
    return finish(me, mine, other, in_hbm(eigvecs), in_hbm(vhi), in_hbm(vlo))


def solution(mesh):
    in_specs = (P("row", "col"), P(None, "row", "col"))
    out_specs = P("row", "col")
    return jax.shard_map(shards, mesh=mesh, in_specs=in_specs, out_specs=out_specs, check_vma=False)
```

```python
import jax
import jax.numpy as jnp
from jax import lax
from jax.experimental import pallas as pl
from jax.experimental.pallas import tpu as pltpu
from jax.sharding import PartitionSpec as P

F32 = jnp.float32
BF16 = jnp.bfloat16
CHIPS = 8
ROWS = 4096
COLS = 128
NV = 512
PARTS = tuple(pl.ds(first, 1024) for first in range(0, ROWS, 1024))
VMEM = 32 * 1024 * 1024
ARRIVAL = ((0, 1), (-1, -2), (2, 3), (-3, -4))


def split(value):
    high = value.astype(BF16)
    low = (value - high.astype(F32)).astype(BF16)
    return high, low


def nt(left, right):
    return lax.dot_general(left, right, (((1,), (1,)), ((), ())), preferred_element_type=F32)


def nn(left, right):
    return lax.dot_general(left, right, (((1,), (0,)), ((), ())), preferred_element_type=F32)


def hidot(left, right):
    return jnp.dot(left, right, precision=lax.Precision.HIGHEST, preferred_element_type=F32)


def assemble(me, index, piece, vhi, vlo):
    chip, core = me // 2, me % 2
    turn = 1 - 2 * ((chip + core) % 2)
    swapped, arrival, block = index // 8, index % 8 // 2, index % 2
    for half in range(2):
        step = ARRIVAL[arrival][half] * (1 - 2 * swapped)
        source = (chip + turn * step + CHIPS) % CHIPS
        column = block * 256 + source * 32 + (1 - core if swapped else core) * 16
        high, low = split(piece[half * 16 : half * 16 + 16, :])
        at = pl.ds(pl.multiple_of(column, 16), 16)
        vhi[at, :] = high
        vlo[at, :] = low


def products_kernel(me, *refs):
    pieces = refs[:16]
    c_hbm, vhi_hbm, vlo_hbm, out, raw, c_ref, vhi, vlo, sums, come, gone, sent = refs[16:]
    core = me[0] % 2
    incoming = [pltpu.make_async_copy(piece, raw.at[n], come.at[n]) for n, piece in enumerate(pieces)]
    for index, at in enumerate(PARTS):
        incoming.append(pltpu.make_async_copy(c_hbm.at[at], c_ref.at[at], come.at[16 + index]))
    for copy in incoming:
        copy.start()
    for n in sorted(range(16), key=lambda n: -(n % 8)):
        incoming[n].wait()
        assemble(me[0], n, raw.at[n], vhi, vlo)
    outgoing = []
    for index, at in enumerate(PARTS):
        for which, (here, there) in enumerate(((vhi, vhi_hbm), (vlo, vlo_hbm))):
            outgoing.append(pltpu.make_async_copy(here.at[:, at], there.at[:, at], gone.at[index, which]))
            outgoing[-1].start()
    for copy in incoming[16:]:
        copy.wait()
    chi, clo = split(c_ref[...])
    both = nn(vhi[...], jnp.concatenate([chi, clo], axis=1))
    proj = both[:, :COLS] + both[:, COLS:] + nn(vlo[...], chi)
    sums[:, :16, :] = proj.reshape(32, 16, COLS)
    outgoing.append(pltpu.make_async_copy(sums.at[:, :16, :], out.at[:, :16, :], sent.at[0]))
    outgoing[-1].start()

    own = pl.ds(pl.multiple_of(core * 256, 256), 256)
    strip = pl.ds(pl.multiple_of(core * 128, 128), 128)
    mixed = nt(vhi[own, :], vlo[own, :])
    square = nt(vhi[own, :], vhi[own, :]) + mixed + mixed.T
    stacked = nt(jnp.concatenate([vhi[strip, :], vlo[strip, :]], axis=0), vhi[256:, :])
    cross = stacked[:128] + stacked[128:] + nt(vhi[strip, :], vlo[256:, :])
    parts = [square[:128, :128], square[:128, 128:], square[128:, 128:], cross[:, :128], cross[:, 128:]]
    parts.append(jnp.zeros((128, 128), F32))
    sums[:, 16:, :] = jnp.concatenate(parts, axis=0).reshape(32, 24, COLS)
    outgoing.append(pltpu.make_async_copy(sums.at[:, 16:, :], out.at[:, 16:, :], sent.at[1]))
    outgoing[-1].start()
    for copy in outgoing:
        copy.wait()


def products(me, pieces, current):
    return pl.pallas_call(
        products_kernel,
        in_specs=[pl.BlockSpec(memory_space=pltpu.SMEM)] + [pl.BlockSpec(memory_space=pl.ANY)] * 17,
        out_specs=[pl.BlockSpec(memory_space=pl.ANY)] * 3,
        out_shape=[
            pltpu.HBM((NV, ROWS), BF16),
            pltpu.HBM((NV, ROWS), BF16),
            jax.ShapeDtypeStruct((32, 40, COLS), F32),
        ],
        scratch_shapes=[
            pltpu.VMEM((16, 32, ROWS), F32),
            pltpu.VMEM((ROWS, COLS), F32),
            pltpu.VMEM((NV, ROWS), BF16),
            pltpu.VMEM((NV, ROWS), BF16),
            pltpu.VMEM((32, 40, COLS), F32),
            pltpu.SemaphoreType.DMA((16 + len(PARTS),)),
            pltpu.SemaphoreType.DMA((len(PARTS), 2)),
            pltpu.SemaphoreType.DMA((2,)),
        ],
        compiler_params=pltpu.CompilerParams(vmem_limit_bytes=VMEM),
        name="products",
    )(me, *pieces, current)


def invert_unit(nilpot):
    row = lax.broadcasted_iota(jnp.int32, (128, 128), 0)
    col = lax.broadcasted_iota(jnp.int32, (128, 128), 1)
    eye = (row == col).astype(F32)
    near = [jnp.where(row // 4 == col // 4, n, 0.0) for n in nilpot]
    square = [hidot(n, n) for n in near]
    inverse = [hidot(eye - n, eye + s) for n, s in zip(near, square)]
    size = 4
    while size < 128:
        pair = (row // (2 * size) == col // (2 * size)) & (row // size != col // size)
        right = [hidot(jnp.where(pair, n, 0.0), r) for n, r in zip(nilpot, inverse)]
        inverse = [r - hidot(r, t) for r, t in zip(inverse, right)]
        size *= 2
    return inverse


def invert_kernel(mine, out, part, come):
    copy = pltpu.make_async_copy(mine.at[:, 16:, :], part, come)
    copy.start()
    copy.wait()
    flat = part[...].reshape(768, 128)
    gram = [flat[:128], flat[128:256], flat[256:384]]
    row = lax.broadcasted_iota(jnp.int32, (128, 128), 0)
    col = lax.broadcasted_iota(jnp.int32, (128, 128), 1)
    diagonal = [jnp.where(row == col, gram[i], 0.0) for i in (0, 2)]
    scale = [2.0 / jnp.sum(d, axis=1, keepdims=True) for d in diagonal]
    across = [2.0 / jnp.sum(d, axis=0, keepdims=True) for d in diagonal]
    upper, lower = invert_unit([jnp.where(row < col, gram[2 * i] * scale[i], 0.0) for i in range(2)])
    corner = hidot(upper, hidot(gram[1] * scale[0], lower))
    out[:128, :] = upper * across[0]
    out[128:256, :] = -corner * across[1]
    out[256:384, :] = lower * across[1]
    out[384:, :] = flat[384:640]


def invert(mine):
    return pl.pallas_call(
        invert_kernel,
        in_specs=[pl.BlockSpec(memory_space=pl.ANY)],
        out_specs=pl.BlockSpec(memory_space=pltpu.VMEM),
        out_shape=jax.ShapeDtypeStruct((640, 128), F32),
        scratch_shapes=[pltpu.VMEM((32, 24, COLS), F32), pltpu.SemaphoreType.DMA],
        compiler_params=pltpu.CompilerParams(vmem_limit_bytes=VMEM),
        name="invert",
    )(mine)


def coefficients(me, project, here, there):
    first_core = me[0] % 2 == 0
    project = project[...].reshape(NV, COLS)
    inverse, cross = [], []
    for block in range(2):
        data = jnp.where(first_core == (block == 0), here[...], there[...])
        upper = jnp.concatenate([data[:128], data[128:256]], axis=1)
        lower = jnp.concatenate([jnp.zeros((128, 128), F32), data[256:384]], axis=1)
        inverse.append(jnp.concatenate([upper, lower], axis=0))
        cross.append(jnp.concatenate([data[384:512], data[512:]], axis=1))
    later = hidot(inverse[1], project[256:])
    earlier = hidot(inverse[0], project[:256] - hidot(jnp.concatenate(cross, axis=0), later))
    return split(jnp.concatenate([earlier, later], axis=0).T)


def finish_kernel(me, mine, here, there, c_hbm, vhi_hbm, vlo_hbm, out, project, first, second, c_ref, vhi, vlo, done, small, come, gone):
    needed = ((mine.at[:, :16, :], project), (here, first), (there, second))
    needed = [pltpu.make_async_copy(*pair, small.at[which]) for which, pair in enumerate(needed)]
    for copy in needed:
        copy.start()
    copies = []
    for index, at in enumerate(PARTS):
        pairs = ((vhi_hbm.at[:, at], vhi.at[:, at]), (vlo_hbm.at[:, at], vlo.at[:, at]), (c_hbm.at[at], c_ref.at[at]))
        copies.append([pltpu.make_async_copy(*pair, come.at[index, which]) for which, pair in enumerate(pairs)])
        for copy in copies[-1]:
            copy.start()
    for copy in needed:
        copy.wait()
    xhi, xlo = coefficients(me, project, first, second)
    both = jnp.concatenate([xhi, xlo], axis=0)
    writes = []
    for index, at in enumerate(PARTS):
        for copy in copies[index]:
            copy.wait()
        wide = nn(both, vhi[:, at])
        change = wide[:COLS] + wide[COLS:] + nn(xhi, vlo[:, at])
        done[at, :] = c_ref[at, :] - change.T
        writes.append(pltpu.make_async_copy(done.at[at], out.at[at], gone.at[index]))
        writes[-1].start()
    for write in writes:
        write.wait()


def finish(me, mine, here, there, current, vhi, vlo):
    return pl.pallas_call(
        finish_kernel,
        in_specs=[pl.BlockSpec(memory_space=pltpu.SMEM)]
        + [pl.BlockSpec(memory_space=pl.ANY)] * 6,
        out_specs=pl.BlockSpec(memory_space=pl.ANY),
        out_shape=jax.ShapeDtypeStruct((ROWS, COLS), F32),
        scratch_shapes=[
            pltpu.VMEM((32, 16, COLS), F32),
            pltpu.VMEM((640, 128), F32),
            pltpu.VMEM((640, 128), F32),
            pltpu.VMEM((ROWS, COLS), F32),
            pltpu.VMEM((NV, ROWS), BF16),
            pltpu.VMEM((NV, ROWS), BF16),
            pltpu.VMEM((ROWS, COLS), F32),
            pltpu.SemaphoreType.DMA((3,)),
            pltpu.SemaphoreType.DMA((len(PARTS), 3)),
            pltpu.SemaphoreType.DMA((len(PARTS),)),
        ],
        compiler_params=pltpu.CompilerParams(vmem_limit_bytes=VMEM),
        name="finish",
    )(me, mine, here, there, current, vhi, vlo)


def exchange(value, side):
    perm = []
    for chip in range(CHIPS):
        for core in range(2):
            turn = 1 if (chip + core) % 2 == 0 else -1
            target = (chip + side * turn) % CHIPS
            perm.append((chip * 2 + core, target * 2 + core))
    return lax.ppermute(value, "col", perm)


def in_hbm(value):
    return pltpu.with_memory_space_constraint(value, pltpu.HBM)


def swap_cores(value):
    return lax.ppermute(value, "col", [(i, i ^ 1) for i in range(2 * CHIPS)])


def shards(eigvecs, householder):
    me = lax.axis_index("col").reshape(1)
    own = householder.transpose(0, 2, 1)
    chains = [own[0], own[1]]
    chains = [jnp.concatenate([piece, exchange(piece, 1)], axis=0) for piece in chains]
    pieces = list(chains)
    for side in (-1, 1, -1):
        chains = [exchange(piece, side) for piece in chains]
        pieces += chains
    pieces += [swap_cores(piece) for piece in pieces]

    vhi, vlo, partial = products(me, [in_hbm(piece) if n % 8 < 4 else piece for n, piece in enumerate(pieces)], in_hbm(eigvecs))
    summed = lax.all_to_all(partial, "row", 0, 0, tiled=True).sum(axis=0)
    mine = lax.all_to_all(jnp.broadcast_to(summed[None], (32, 40, COLS)), "row", 0, 0, tiled=True)
    here = invert(mine)
    return finish(me, mine, here, swap_cores(here), in_hbm(eigvecs), in_hbm(vhi), in_hbm(vlo))


def solution(mesh):
    in_specs = (P("row", "col"), P(None, "row", "col"))
    out_specs = P("row", "col")
    return jax.shard_map(shards, mesh=mesh, in_specs=in_specs, out_specs=out_specs, check_vma=False)
```

```python
import jax
import jax.numpy as jnp
from jax import lax
from jax.experimental import pallas as pl
from jax.experimental.pallas import tpu as pltpu
from jax.sharding import PartitionSpec as P

F32 = jnp.float32
BF16 = jnp.bfloat16
CHIPS = 8
ROWS = 4096
COLS = 128
NV = 512
PARTS = tuple(pl.ds(first, 1024) for first in range(0, ROWS, 1024))
VMEM = 32 * 1024 * 1024
ARRIVAL = ((0, 1), (-1, -2), (2, 3), (-3, -4))


def split(value):
    high = value.astype(BF16)
    low = (value - high.astype(F32)).astype(BF16)
    return high, low


def nt(left, right):
    return lax.dot_general(left, right, (((1,), (1,)), ((), ())), preferred_element_type=F32)


def nn(left, right):
    return lax.dot_general(left, right, (((1,), (0,)), ((), ())), preferred_element_type=F32)


def hidot(left, right):
    return jnp.dot(left, right, precision=lax.Precision.HIGHEST, preferred_element_type=F32)


def assemble(me, index, piece, vhi, vlo):
    chip, core = me // 2, me % 2
    turn = 1 - 2 * ((chip + core) % 2)
    swapped, arrival, block = index // 8, index % 8 // 2, index % 2
    for half in range(2):
        step = ARRIVAL[arrival][half] * (1 - 2 * swapped)
        source = (chip + turn * step + CHIPS) % CHIPS
        column = block * 256 + source * 32 + (1 - core if swapped else core) * 16
        high, low = split(piece[half * 16 : half * 16 + 16, :])
        at = pl.ds(pl.multiple_of(column, 16), 16)
        vhi[at, :] = high
        vlo[at, :] = low


def products_kernel(me, *refs):
    pieces = refs[:16]
    c_hbm, vhi_hbm, vlo_hbm, out, raw, c_ref, vhi, vlo, come, gone = refs[16:]
    core = me[0] % 2
    incoming = [pltpu.make_async_copy(piece, raw.at[n], come.at[n]) for n, piece in enumerate(pieces)]
    for index, at in enumerate(PARTS):
        incoming.append(pltpu.make_async_copy(c_hbm.at[at], c_ref.at[at], come.at[16 + index]))
    for copy in incoming:
        copy.start()
    for n in sorted(range(16), key=lambda n: -(n % 8)):
        incoming[n].wait()
        assemble(me[0], n, raw.at[n], vhi, vlo)
    outgoing = []
    for index, at in enumerate(PARTS):
        for which, (here, there) in enumerate(((vhi, vhi_hbm), (vlo, vlo_hbm))):
            outgoing.append(pltpu.make_async_copy(here.at[:, at], there.at[:, at], gone.at[index, which]))
            outgoing[-1].start()
    for copy in incoming[16:]:
        copy.wait()
    chi, clo = split(c_ref[...])
    both = nn(vhi[...], jnp.concatenate([chi, clo], axis=1))
    proj = both[:, :COLS] + both[:, COLS:] + nn(vlo[...], chi)
    out[:, :16, :] = proj.reshape(32, 16, COLS)

    own = pl.ds(pl.multiple_of(core * 256, 256), 256)
    strip = pl.ds(pl.multiple_of(core * 128, 128), 128)
    mixed = nt(vhi[own, :], vlo[own, :])
    square = nt(vhi[own, :], vhi[own, :]) + mixed + mixed.T
    stacked = nt(jnp.concatenate([vhi[strip, :], vlo[strip, :]], axis=0), vhi[256:, :])
    cross = stacked[:128] + stacked[128:] + nt(vhi[strip, :], vlo[256:, :])
    parts = [square[:128, :128], square[:128, 128:], square[128:, 128:], cross[:, :128], cross[:, 128:]]
    parts.append(jnp.zeros((128, 128), F32))
    out[:, 16:, :] = jnp.concatenate(parts, axis=0).reshape(32, 24, COLS)

    for copy in outgoing:
        copy.wait()


def products(me, pieces, current):
    return pl.pallas_call(
        products_kernel,
        in_specs=[pl.BlockSpec(memory_space=pltpu.SMEM)] + [pl.BlockSpec(memory_space=pl.ANY)] * 17,
        out_specs=[pl.BlockSpec(memory_space=pl.ANY)] * 2 + [pl.BlockSpec(memory_space=pltpu.VMEM)],
        out_shape=[
            pltpu.HBM((NV, ROWS), BF16),
            pltpu.HBM((NV, ROWS), BF16),
            jax.ShapeDtypeStruct((32, 40, COLS), F32),
        ],
        scratch_shapes=[
            pltpu.VMEM((16, 32, ROWS), F32),
            pltpu.VMEM((ROWS, COLS), F32),
            pltpu.VMEM((NV, ROWS), BF16),
            pltpu.VMEM((NV, ROWS), BF16),
            pltpu.SemaphoreType.DMA((16 + len(PARTS),)),
            pltpu.SemaphoreType.DMA((len(PARTS), 2)),
        ],
        compiler_params=pltpu.CompilerParams(vmem_limit_bytes=VMEM),
        name="products",
    )(me, *pieces, current)


def invert_unit(nilpot):
    row = lax.broadcasted_iota(jnp.int32, (128, 128), 0)
    col = lax.broadcasted_iota(jnp.int32, (128, 128), 1)
    eye = (row == col).astype(F32)
    near = [jnp.where(row // 4 == col // 4, n, 0.0) for n in nilpot]
    square = [hidot(n, n) for n in near]
    inverse = [hidot(eye - n, eye + s) for n, s in zip(near, square)]
    size = 4
    while size < 128:
        pair = (row // (2 * size) == col // (2 * size)) & (row // size != col // size)
        right = [hidot(jnp.where(pair, n, 0.0), r) for n, r in zip(nilpot, inverse)]
        inverse = [r - hidot(r, t) for r, t in zip(inverse, right)]
        size *= 2
    return inverse


def invert_kernel(mine, out, part, come):
    copy = pltpu.make_async_copy(mine.at[:, 16:, :], part, come)
    copy.start()
    copy.wait()
    flat = part[...].reshape(768, 128)
    gram = [flat[:128], flat[128:256], flat[256:384]]
    row = lax.broadcasted_iota(jnp.int32, (128, 128), 0)
    col = lax.broadcasted_iota(jnp.int32, (128, 128), 1)
    diagonal = [jnp.where(row == col, gram[i], 0.0) for i in (0, 2)]
    scale = [2.0 / jnp.sum(d, axis=1, keepdims=True) for d in diagonal]
    across = [2.0 / jnp.sum(d, axis=0, keepdims=True) for d in diagonal]
    upper, lower = invert_unit([jnp.where(row < col, gram[2 * i] * scale[i], 0.0) for i in range(2)])
    corner = hidot(upper, hidot(gram[1] * scale[0], lower))
    out[:128, :] = upper * across[0]
    out[128:256, :] = -corner * across[1]
    out[256:384, :] = lower * across[1]
    out[384:, :] = flat[384:640]


def invert(mine):
    return pl.pallas_call(
        invert_kernel,
        in_specs=[pl.BlockSpec(memory_space=pl.ANY)],
        out_specs=pl.BlockSpec(memory_space=pltpu.VMEM),
        out_shape=jax.ShapeDtypeStruct((640, 128), F32),
        scratch_shapes=[pltpu.VMEM((32, 24, COLS), F32), pltpu.SemaphoreType.DMA],
        compiler_params=pltpu.CompilerParams(vmem_limit_bytes=VMEM),
        name="invert",
    )(mine)


def coefficients(me, project, here, there):
    first_core = me[0] % 2 == 0
    project = project[...].reshape(NV, COLS)
    inverse, cross = [], []
    for block in range(2):
        data = jnp.where(first_core == (block == 0), here[...], there[...])
        upper = jnp.concatenate([data[:128], data[128:256]], axis=1)
        lower = jnp.concatenate([jnp.zeros((128, 128), F32), data[256:384]], axis=1)
        inverse.append(jnp.concatenate([upper, lower], axis=0))
        cross.append(jnp.concatenate([data[384:512], data[512:]], axis=1))
    later = hidot(inverse[1], project[256:])
    earlier = hidot(inverse[0], project[:256] - hidot(jnp.concatenate(cross, axis=0), later))
    return split(jnp.concatenate([earlier, later], axis=0).T)


def finish_kernel(me, mine, here, there, c_hbm, vhi_hbm, vlo_hbm, out, project, first, second, c_ref, vhi, vlo, done, small, come, gone):
    needed = ((mine.at[:, :16, :], project), (here, first), (there, second))
    needed = [pltpu.make_async_copy(*pair, small.at[which]) for which, pair in enumerate(needed)]
    for copy in needed:
        copy.start()
    copies = []
    for index, at in enumerate(PARTS):
        pairs = ((vhi_hbm.at[:, at], vhi.at[:, at]), (vlo_hbm.at[:, at], vlo.at[:, at]), (c_hbm.at[at], c_ref.at[at]))
        copies.append([pltpu.make_async_copy(*pair, come.at[index, which]) for which, pair in enumerate(pairs)])
        for copy in copies[-1]:
            copy.start()
    for copy in needed:
        copy.wait()
    xhi, xlo = coefficients(me, project, first, second)
    both = jnp.concatenate([xhi, xlo], axis=0)
    writes = []
    for index, at in enumerate(PARTS):
        for copy in copies[index]:
            copy.wait()
        wide = nn(both, vhi[:, at])
        change = wide[:COLS] + wide[COLS:] + nn(xhi, vlo[:, at])
        done[at, :] = c_ref[at, :] - change.T
        writes.append(pltpu.make_async_copy(done.at[at], out.at[at], gone.at[index]))
        writes[-1].start()
    for write in writes:
        write.wait()


def finish(me, mine, here, there, current, vhi, vlo):
    return pl.pallas_call(
        finish_kernel,
        in_specs=[pl.BlockSpec(memory_space=pltpu.SMEM)]
        + [pl.BlockSpec(memory_space=pl.ANY)] * 6,
        out_specs=pl.BlockSpec(memory_space=pl.ANY),
        out_shape=jax.ShapeDtypeStruct((ROWS, COLS), F32),
        scratch_shapes=[
            pltpu.VMEM((32, 16, COLS), F32),
            pltpu.VMEM((640, 128), F32),
            pltpu.VMEM((640, 128), F32),
            pltpu.VMEM((ROWS, COLS), F32),
            pltpu.VMEM((NV, ROWS), BF16),
            pltpu.VMEM((NV, ROWS), BF16),
            pltpu.VMEM((ROWS, COLS), F32),
            pltpu.SemaphoreType.DMA((3,)),
            pltpu.SemaphoreType.DMA((len(PARTS), 3)),
            pltpu.SemaphoreType.DMA((len(PARTS),)),
        ],
        compiler_params=pltpu.CompilerParams(vmem_limit_bytes=VMEM),
        name="finish",
    )(me, mine, here, there, current, vhi, vlo)


def exchange(value, side):
    perm = []
    for chip in range(CHIPS):
        for core in range(2):
            turn = 1 if (chip + core) % 2 == 0 else -1
            target = (chip + side * turn) % CHIPS
            perm.append((chip * 2 + core, target * 2 + core))
    return lax.ppermute(value, "col", perm)


def in_hbm(value):
    return pltpu.with_memory_space_constraint(value, pltpu.HBM)


def swap_cores(value):
    return lax.ppermute(value, "col", [(i, i ^ 1) for i in range(2 * CHIPS)])


def shards(eigvecs, householder):
    me = lax.axis_index("col").reshape(1)
    own = householder.transpose(0, 2, 1)
    chains = [own[0], own[1]]
    chains = [jnp.concatenate([piece, exchange(piece, 1)], axis=0) for piece in chains]
    pieces = list(chains)
    for side in (-1, 1, -1):
        chains = [exchange(piece, side) for piece in chains]
        pieces += chains
    pieces += [swap_cores(piece) for piece in pieces]

    vhi, vlo, partial = products(me, [in_hbm(piece) if n % 8 < 4 else piece for n, piece in enumerate(pieces)], in_hbm(eigvecs))
    summed = lax.all_to_all(partial, "row", 0, 0, tiled=True).sum(axis=0)
    mine = lax.all_to_all(jnp.broadcast_to(summed[None], (32, 40, COLS)), "row", 0, 0, tiled=True)
    here = invert(mine)
    return finish(me, mine, here, swap_cores(here), in_hbm(eigvecs), in_hbm(vhi), in_hbm(vlo))


def solution(mesh):
    in_specs = (P("row", "col"), P(None, "row", "col"))
    out_specs = P("row", "col")
    return jax.shard_map(shards, mesh=mesh, in_specs=in_specs, out_specs=out_specs, check_vma=False)
```

```python
import jax
import jax.numpy as jnp
from jax import lax
from jax.experimental import pallas as pl
from jax.experimental.pallas import tpu as pltpu
from jax.sharding import PartitionSpec as P

F32 = jnp.float32
BF16 = jnp.bfloat16
CHIPS = 8
ROWS = 4096
COLS = 128
NV = 512
PARTS = tuple(pl.ds(first, 1024) for first in range(0, ROWS, 1024))
VMEM = 32 * 1024 * 1024
ARRIVAL = ((0, 1), (-1, -2), (2, 3), (-3, -4))


def split(value):
    high = value.astype(BF16)
    low = (value - high.astype(F32)).astype(BF16)
    return high, low


def nt(left, right):
    return lax.dot_general(left, right, (((1,), (1,)), ((), ())), preferred_element_type=F32)


def nn(left, right):
    return lax.dot_general(left, right, (((1,), (0,)), ((), ())), preferred_element_type=F32)


def hidot(left, right):
    return jnp.dot(left, right, precision=lax.Precision.HIGHEST, preferred_element_type=F32)


def assemble(me, index, piece, vhi, vlo):
    chip, core = me // 2, me % 2
    turn = 1 - 2 * ((chip + core) % 2)
    swapped, arrival, block = index // 8, index % 8 // 2, index % 2
    for half in range(2):
        step = ARRIVAL[arrival][half] * (1 - 2 * swapped)
        source = (chip + turn * step + CHIPS) % CHIPS
        column = block * 256 + source * 32 + (1 - core if swapped else core) * 16
        high, low = split(piece[half * 16 : half * 16 + 16, :])
        at = pl.ds(pl.multiple_of(column, 16), 16)
        vhi[at, :] = high
        vlo[at, :] = low


def products_kernel(me, *refs):
    pieces = refs[:16]
    c_hbm, vhi_hbm, vlo_hbm, out, raw, c_ref, vhi, vlo, come, gone = refs[16:]
    core = me[0] % 2
    incoming = [pltpu.make_async_copy(piece, raw.at[n], come.at[n]) for n, piece in enumerate(pieces)]
    for index, at in enumerate(PARTS):
        incoming.append(pltpu.make_async_copy(c_hbm.at[at], c_ref.at[at], come.at[16 + index]))
    for copy in incoming:
        copy.start()
    for n in sorted(range(16), key=lambda n: -(n % 8)):
        incoming[n].wait()
        assemble(me[0], n, raw.at[n], vhi, vlo)
    outgoing = []
    for index, at in enumerate(PARTS):
        for which, (here, there) in enumerate(((vhi, vhi_hbm), (vlo, vlo_hbm))):
            outgoing.append(pltpu.make_async_copy(here.at[:, at], there.at[:, at], gone.at[index, which]))
            outgoing[-1].start()
    for copy in incoming[16:]:
        copy.wait()
    chi, clo = split(c_ref[...])
    both = nn(vhi[...], jnp.concatenate([chi, clo], axis=1))
    proj = both[:, :COLS] + both[:, COLS:] + nn(vlo[...], chi)
    out[:, :16, :] = proj.reshape(32, 16, COLS)

    own = pl.ds(pl.multiple_of(core * 256, 256), 256)
    strip = pl.ds(pl.multiple_of(core * 128, 128), 128)
    mixed = nt(vhi[own, :], vlo[own, :])
    square = nt(vhi[own, :], vhi[own, :]) + mixed + mixed.T
    stacked = nt(jnp.concatenate([vhi[strip, :], vlo[strip, :]], axis=0), vhi[256:, :])
    cross = stacked[:128] + stacked[128:] + nt(vhi[strip, :], vlo[256:, :])
    parts = [square[:128, :128], square[:128, 128:], square[128:, 128:], cross[:, :128], cross[:, 128:]]
    parts.append(jnp.zeros((128, 128), F32))
    out[:, 16:, :] = jnp.concatenate(parts, axis=0).reshape(32, 24, COLS)

    for copy in outgoing:
        copy.wait()


def products(me, pieces, current):
    return pl.pallas_call(
        products_kernel,
        in_specs=[pl.BlockSpec(memory_space=pltpu.SMEM)] + [pl.BlockSpec(memory_space=pl.ANY)] * 17,
        out_specs=[pl.BlockSpec(memory_space=pl.ANY)] * 2 + [pl.BlockSpec(memory_space=pltpu.VMEM)],
        out_shape=[
            pltpu.HBM((NV, ROWS), BF16),
            pltpu.HBM((NV, ROWS), BF16),
            jax.ShapeDtypeStruct((32, 40, COLS), F32),
        ],
        scratch_shapes=[
            pltpu.VMEM((16, 32, ROWS), F32),
            pltpu.VMEM((ROWS, COLS), F32),
            pltpu.VMEM((NV, ROWS), BF16),
            pltpu.VMEM((NV, ROWS), BF16),
            pltpu.SemaphoreType.DMA((16 + len(PARTS),)),
            pltpu.SemaphoreType.DMA((len(PARTS), 2)),
        ],
        compiler_params=pltpu.CompilerParams(vmem_limit_bytes=VMEM),
        name="products",
    )(me, *pieces, current)


def invert_unit(nilpot):
    row = lax.broadcasted_iota(jnp.int32, (128, 128), 0)
    col = lax.broadcasted_iota(jnp.int32, (128, 128), 1)
    eye = (row == col).astype(F32)
    near = [jnp.where(row // 4 == col // 4, n, 0.0) for n in nilpot]
    square = [hidot(n, n) for n in near]
    inverse = [hidot(eye - n, eye + s) for n, s in zip(near, square)]
    size = 4
    while size < 128:
        pair = (row // (2 * size) == col // (2 * size)) & (row // size != col // size)
        right = [hidot(jnp.where(pair, n, 0.0), r) for n, r in zip(nilpot, inverse)]
        inverse = [r - hidot(r, t) for r, t in zip(inverse, right)]
        size *= 2
    return inverse


def invert_kernel(mine, out, part, come):
    copy = pltpu.make_async_copy(mine.at[:, 16:, :], part, come)
    copy.start()
    copy.wait()
    flat = part[...].reshape(768, 128)
    gram = [flat[:128], flat[128:256], flat[256:384]]
    row = lax.broadcasted_iota(jnp.int32, (128, 128), 0)
    col = lax.broadcasted_iota(jnp.int32, (128, 128), 1)
    diagonal = [jnp.where(row == col, gram[i], 0.0) for i in (0, 2)]
    scale = [2.0 / jnp.sum(d, axis=1, keepdims=True) for d in diagonal]
    across = [2.0 / jnp.sum(d, axis=0, keepdims=True) for d in diagonal]
    upper, lower = invert_unit([jnp.where(row < col, gram[2 * i] * scale[i], 0.0) for i in range(2)])
    corner = hidot(upper, hidot(gram[1] * scale[0], lower))
    out[:128, :] = upper * across[0]
    out[128:256, :] = -corner * across[1]
    out[256:384, :] = lower * across[1]
    out[384:, :] = flat[384:640]


def invert(mine):
    return pl.pallas_call(
        invert_kernel,
        in_specs=[pl.BlockSpec(memory_space=pl.ANY)],
        out_specs=pl.BlockSpec(memory_space=pltpu.VMEM),
        out_shape=jax.ShapeDtypeStruct((640, 128), F32),
        scratch_shapes=[pltpu.VMEM((32, 24, COLS), F32), pltpu.SemaphoreType.DMA],
        compiler_params=pltpu.CompilerParams(vmem_limit_bytes=VMEM),
        name="invert",
    )(mine)


def coefficients(me, project, here, there):
    first_core = me[0] % 2 == 0
    project = project[...].reshape(NV, COLS)
    inverse, cross = [], []
    for block in range(2):
        data = jnp.where(first_core == (block == 0), here[...], there[...])
        upper = jnp.concatenate([data[:128], data[128:256]], axis=1)
        lower = jnp.concatenate([jnp.zeros((128, 128), F32), data[256:384]], axis=1)
        inverse.append(jnp.concatenate([upper, lower], axis=0))
        cross.append(jnp.concatenate([data[384:512], data[512:]], axis=1))
    later = hidot(inverse[1], project[256:])
    earlier = hidot(inverse[0], project[:256] - hidot(jnp.concatenate(cross, axis=0), later))
    return split(jnp.concatenate([earlier, later], axis=0).T)


def finish_kernel(me, mine, here, there, c_hbm, vhi_hbm, vlo_hbm, out, project, first, second, c_ref, vhi, vlo, done, small, come, gone):
    needed = ((mine.at[:, :16, :], project), (here, first), (there, second))
    needed = [pltpu.make_async_copy(*pair, small.at[which]) for which, pair in enumerate(needed)]
    for copy in needed:
        copy.start()
    copies = []
    for index, at in enumerate(PARTS):
        pairs = ((vhi_hbm.at[:, at], vhi.at[:, at]), (vlo_hbm.at[:, at], vlo.at[:, at]), (c_hbm.at[at], c_ref.at[at]))
        copies.append([pltpu.make_async_copy(*pair, come.at[index, which]) for which, pair in enumerate(pairs)])
        for copy in copies[-1]:
            copy.start()
    for copy in needed:
        copy.wait()
    xhi, xlo = coefficients(me, project, first, second)
    both = jnp.concatenate([xhi, xlo], axis=0)
    writes = []
    for index, at in enumerate(PARTS):
        for copy in copies[index]:
            copy.wait()
        wide = nn(both, vhi[:, at])
        change = wide[:COLS] + wide[COLS:] + nn(xhi, vlo[:, at])
        done[at, :] = c_ref[at, :] - change.T
        writes.append(pltpu.make_async_copy(done.at[at], out.at[at], gone.at[index]))
        writes[-1].start()
    for write in writes:
        write.wait()


def finish(me, mine, here, there, current, vhi, vlo):
    return pl.pallas_call(
        finish_kernel,
        in_specs=[pl.BlockSpec(memory_space=pltpu.SMEM)]
        + [pl.BlockSpec(memory_space=pl.ANY)] * 6,
        out_specs=pl.BlockSpec(memory_space=pl.ANY),
        out_shape=jax.ShapeDtypeStruct((ROWS, COLS), F32),
        scratch_shapes=[
            pltpu.VMEM((32, 16, COLS), F32),
            pltpu.VMEM((640, 128), F32),
            pltpu.VMEM((640, 128), F32),
            pltpu.VMEM((ROWS, COLS), F32),
            pltpu.VMEM((NV, ROWS), BF16),
            pltpu.VMEM((NV, ROWS), BF16),
            pltpu.VMEM((ROWS, COLS), F32),
            pltpu.SemaphoreType.DMA((3,)),
            pltpu.SemaphoreType.DMA((len(PARTS), 3)),
            pltpu.SemaphoreType.DMA((len(PARTS),)),
        ],
        compiler_params=pltpu.CompilerParams(vmem_limit_bytes=VMEM),
        name="finish",
    )(me, mine, here, there, current, vhi, vlo)


def exchange(value, side):
    perm = []
    for chip in range(CHIPS):
        for core in range(2):
            turn = 1 if (chip + core) % 2 == 0 else -1
            target = (chip + side * turn) % CHIPS
            perm.append((chip * 2 + core, target * 2 + core))
    return lax.ppermute(value, "col", perm)


def in_hbm(value):
    return pltpu.with_memory_space_constraint(value, pltpu.HBM)


def swap_cores(value):
    return lax.ppermute(value, "col", [(i, i ^ 1) for i in range(2 * CHIPS)])


def shards(eigvecs, householder):
    me = lax.axis_index("col").reshape(1)
    own = householder.transpose(0, 2, 1)
    chains = [own[0], own[1]]
    chains = [jnp.concatenate([piece, exchange(piece, 1)], axis=0) for piece in chains]
    pieces = list(chains)
    for side in (-1, 1, -1):
        chains = [exchange(piece, side) for piece in chains]
        pieces += chains
    pieces += [swap_cores(piece) for piece in pieces]

    vhi, vlo, partial = products(me, [in_hbm(piece) if n % 8 < 4 else piece for n, piece in enumerate(pieces)], in_hbm(eigvecs))
    summed = lax.all_to_all(partial, "row", 0, 0, tiled=True).sum(axis=0)
    mine = lax.all_to_all(jnp.broadcast_to(summed[None], (32, 40, COLS)), "row", 0, 0, tiled=True)
    here = invert(mine)
    return finish(me, mine, here, swap_cores(here), eigvecs, in_hbm(vhi), in_hbm(vlo))


def solution(mesh):
    in_specs = (P("row", "col"), P(None, "row", "col"))
    out_specs = P("row", "col")
    return jax.shard_map(shards, mesh=mesh, in_specs=in_specs, out_specs=out_specs, check_vma=False)
```
